32 devices in a mesh: grp: 8 (over y, x, core), band: 4 (over z).
Axes of the slice: x: 2, y: 2, z: 4, core: 2. Of those that a mesh axis runs over, the one named last changes fastest.
Arguments:
- voltages: bfloat16 [64, 2048, 2048], P('band', 'grp'), may hold values from -6 to 6
- steering: int32 [2, 1024], replicated, may hold values from 0 to 255, as said below
- chan_sub: int32 [1024], P('band'), may hold values from 0 to 15, as said below
- delays: int32 [512, 16], P(None, 'band'), may hold values from 0 to 63
Outputs:
- dedispersed: float32 [64, 1024, 512], P(None, 'grp', 'band')
The draws below stay inside these ranges and needn't reach their ends.
Inputs may be any that keep to these rules, and one draw needn't show every extreme that they name: Every pair (steering[0, b], steering[1, b]) with the first below 256 and the second below 4 occurs for exactly one beam b. chan_sub[c] // 4 == c // 256: a channel belongs to a subband of its own quarter of the band.
All inputs are finite; a program needn't handle non-finite values.
Results may differ from the reference program's by a relative error of at most 0.0041.
Values may be sent and summed in bfloat16 or wider, within the bound.
A program may use at most 128 MiB of HBM per device.

```python
import math
import jax
import jax.numpy as jnp
from jax import lax

A = 2048
FEEDS = 1024
NS_FEEDS = 256
C = 1024
SAMP = 2048
BEAMS = 1024
TRIALS = 512
SUB = 16
FR = 64
CQ = 256
SUBQ = 4


def draw_steering(key, part):
    shuffled = jax.random.permutation(key, BEAMS).astype(jnp.int32)
    north_ids = shuffled % NS_FEEDS
    east_ids = shuffled // NS_FEEDS % 4
    return jnp.stack([north_ids, east_ids]).astype(jnp.int32)


def draw_chan_sub(key, part):
    quarter_base = jnp.arange(C, dtype=jnp.int32) // CQ * SUBQ
    offsets = jax.random.randint(key, (C,), 0, SUBQ, dtype=jnp.int32)
    return (quarter_base + offsets).astype(jnp.int32)


def plant(array, key, smallest, top_value):
    place = [jax.random.randint(jax.random.fold_in(key, axis), (), 0, length) for axis, length in enumerate(array.shape)]
    widest = array.shape.index(max(array.shape))
    neighbour = place[:widest] + [(place[widest] + 1) % array.shape[widest]] + place[widest + 1:]
    return array.at[tuple(place)].set(smallest).at[tuple(neighbour)].set(top_value)


def block_scale(key, extent, pieces, smallest, top_value):
    factor_of, own = 1.0, jax.random.fold_in(key, 6)
    for position, blocks in pieces:
        draws = jnp.exp(jax.random.uniform(jax.random.fold_in(own, position), (blocks,), jnp.float32, smallest / len(pieces), top_value / len(pieces)))
        factor_of = factor_of * jnp.repeat(draws, extent[position] // blocks).reshape([-1 if axis == position else 1 for axis in range(len(extent))])
    return factor_of


def noise(key, shape, width, most, split=(), kind=jnp.bfloat16):
    gain = block_scale(key, shape, split, -0.22, 0.18) if split else 1.0
    result = jax.random.normal(key, shape, jnp.float32) * width * gain
    return jnp.minimum(jnp.maximum(result, -most), most).astype(kind)


def setup_inputs(seed: int = 0) -> dict:
    seeds = jax.random.split(jax.random.key(seed), 5)
    voltages = noise(seeds[0], (FR, A, SAMP), 1.0, 6.0, ((0, 4), (1, 8)))
    steering = draw_steering(jax.random.fold_in(seeds[4], 71), 0)
    chan_sub = draw_chan_sub(jax.random.fold_in(seeds[4], 71), 0)
    delays = plant(jax.random.randint(seeds[3], (TRIALS, SUB), 0, FR), jax.random.fold_in(seeds[3], 1), 0, FR - 1).astype(jnp.int32)
    return dict(voltages=voltages, steering=steering, chan_sub=chan_sub, delays=delays)


def window_taps():
    tap_pos = jnp.arange(4 * SAMP, dtype=jnp.float32) + 0.5
    hann_taper = 0.5 - 0.5 * jnp.cos(2.0 * math.pi / (4 * SAMP) * tap_pos)
    window = hann_taper * jnp.sinc((tap_pos - 2 * SAMP) / SAMP)
    window = window * jnp.sqrt(SAMP / jnp.sum(window * window))
    return window.reshape(4, SAMP)

def dft_table():
    row_ids = jnp.arange(SAMP, dtype=jnp.int32)
    col_ids = jnp.arange(SAMP, dtype=jnp.int32)
    chan_ids = row_ids % C
    phase_steps = chan_ids[:, None] * col_ids[None, :] % SAMP
    angles = 2.0 * math.pi / SAMP * phase_steps.astype(jnp.float32)
    row_scale = 1.0 / math.sqrt(SAMP)
    table = jnp.where((row_ids < C)[:, None], jnp.cos(angles), -jnp.sin(angles)) * row_scale
    return table.astype(jnp.bfloat16)

def beam_weights(channel_at, steering):
    feed_ids = jnp.arange(FEEDS, dtype=jnp.int32)
    north_pos = (feed_ids % NS_FEEDS).astype(jnp.float32) / NS_FEEDS
    east_pos = (feed_ids // NS_FEEDS).astype(jnp.float32) / 4.0
    geometry = north_pos[:, None] * steering[0][None, :].astype(jnp.float32) + east_pos[:, None] * steering[1][None, :].astype(jnp.float32)
    frequency = 1.0 - channel_at.astype(jnp.float32) / (2 * C)
    phases = 2.0 * math.pi * frequency * geometry
    weight_norm = 1.0 / math.sqrt(FEEDS)
    return jnp.concatenate([jnp.cos(phases) * weight_norm, jnp.sin(phases) * weight_norm], axis=1).astype(jnp.bfloat16)

def intensity(channel_block, weights):
    frames = channel_block.shape[1]
    input_rows = channel_block.reshape(4 * frames, FEEDS)
    products = jnp.dot(input_rows, weights, preferred_element_type=jnp.float32).reshape(2, frames, 2, 2, BEAMS)
    beam_re = products[0, :, :, 0] - products[1, :, :, 1]
    beam_im = products[0, :, :, 1] + products[1, :, :, 0]
    return lax.optimization_barrier(jnp.sum(beam_re * beam_re + beam_im * beam_im, axis=1)).astype(jnp.bfloat16)

def fourier_tables(total_frames):
    half_frames = total_frames // 2
    freq_ids = jnp.arange(1, half_frames + 1, dtype=jnp.int32)
    time_ids = jnp.arange(total_frames, dtype=jnp.int32)
    angles = 2.0 * math.pi / total_frames * (freq_ids[:, None] * time_ids[None, :] % total_frames).astype(jnp.float32)
    cosines = jnp.cos(angles)
    sines = jnp.sin(angles)
    forward = jnp.concatenate([cosines, -sines], axis=0)
    weight = jnp.where(freq_ids == half_frames, 1.0, 2.0).astype(jnp.float32) / (total_frames * math.sqrt(C))
    inverse = jnp.transpose(jnp.concatenate([cosines * weight[:, None], -sines * weight[:, None]], axis=0))
    return (forward, inverse)

def trial_phases(delays, total_frames):
    freq_ids = jnp.arange(1, total_frames // 2 + 1, dtype=jnp.int32)
    phase_steps = freq_ids[:, None, None] * jnp.transpose(delays)[None, :, :] % total_frames
    angles = 2.0 * math.pi / total_frames * phase_steps.astype(jnp.float32)
    return (jnp.cos(angles), jnp.sin(angles))

def dedisperse(centered, delays, total_frames):
    highest = lax.Precision.HIGHEST
    forward, inverse = fourier_tables(total_frames)
    half_frames = total_frames // 2
    spectrum = jnp.einsum('km,smb->ksb', forward, centered, precision=highest)
    spec_re = spectrum[:half_frames]
    spec_im = spectrum[half_frames:]
    cosines, sines = trial_phases(delays, total_frames)
    shifted_re = jnp.einsum('ksb,ksd->kbd', spec_re, cosines, precision=highest) + jnp.einsum('ksb,ksd->kbd', spec_im, sines, precision=highest)
    shifted_im = jnp.einsum('ksb,ksd->kbd', spec_im, cosines, precision=highest) - jnp.einsum('ksb,ksd->kbd', spec_re, sines, precision=highest)
    stacked = jnp.concatenate([shifted_re, shifted_im], axis=0)
    beams_here = centered.shape[2]
    trials_all = delays.shape[0]
    flattened = jnp.dot(inverse, stacked.reshape(2 * half_frames, beams_here * trials_all), precision=highest, preferred_element_type=jnp.float32)
    return flattened.reshape(total_frames, beams_here, trials_all)

def reference(voltages, steering, chan_sub, delays):
    total_frames = voltages.shape[0]
    window = window_taps()
    table = dft_table()
    padded = jnp.concatenate([jnp.zeros((3, A, SAMP), voltages.dtype), voltages], axis=0)

    def one_frame(frame_at):
        piece = lax.dynamic_slice_in_dim(padded, frame_at, 4, 0).astype(jnp.float32)
        filtered = window[0][None, :] * piece[0]
        for tap_at in range(1, 4):
            filtered = filtered + window[tap_at][None, :] * piece[tap_at]
        return lax.dot_general(table, filtered.astype(jnp.bfloat16), (((1,), (1,)), ((), ())), preferred_element_type=jnp.float32).astype(jnp.bfloat16)
    spectra = lax.map(one_frame, jnp.arange(total_frames, dtype=jnp.int32))

    def one_channel(channel_at):
        real_rows = lax.dynamic_index_in_dim(spectra, channel_at, 1, keepdims=False)
        imag_rows = lax.dynamic_index_in_dim(spectra, channel_at + C, 1, keepdims=False)
        channel_block = jnp.stack([real_rows, imag_rows])
        return intensity(channel_block, beam_weights(channel_at, steering))
    beam_power = lax.map(one_channel, jnp.arange(C, dtype=jnp.int32))
    member = (chan_sub[:, None] == jnp.arange(SUB, dtype=jnp.int32)[None, :]).astype(jnp.bfloat16)
    band_sums = jnp.dot(jnp.transpose(member), beam_power.reshape(C, total_frames * BEAMS), preferred_element_type=jnp.float32)
    band_sums = band_sums.reshape(SUB, total_frames, BEAMS)
    centered = band_sums - lax.optimization_barrier(jnp.mean(band_sums, axis=1, keepdims=True))
    return dedisperse(centered, delays, total_frames)
```

```python
import math

import jax
import jax.numpy as jnp
from jax import lax
from jax.sharding import PartitionSpec as P

A = 2048
FEEDS = 1024
NS_FEEDS = 256
EW_FEEDS = 4
C = 1024
SAMP = 2048
BEAMS = 1024
QUARTERS = 4
POLS = 2
GROUP_FRAMES = 4


def shifted(block, axis, distance):
    devices = range(lax.axis_size(axis))
    route = [(i - distance, i) for i in devices if i - distance in devices]
    return lax.ppermute(block, axis, route)


def window_taps():
    tap_pos = jnp.arange(4 * SAMP, dtype=jnp.float32) + 0.5
    hann_taper = 0.5 - 0.5 * jnp.cos(2.0 * math.pi / (4 * SAMP) * tap_pos)
    window = hann_taper * jnp.sinc((tap_pos - 2 * SAMP) / SAMP)
    window = window * jnp.sqrt(SAMP / jnp.sum(window * window))
    return window.reshape(4, SAMP)


def unit_circle(steps, whole):
    angles = 2.0 * math.pi / whole * (steps % whole).astype(jnp.float32)
    return (jnp.cos(angles), jnp.sin(angles))


def dft_rows(first_channel, count):
    low = 32
    col_ids = jnp.arange(SAMP, dtype=jnp.int32)[None, :]
    hi_ids = first_channel + low * jnp.arange(count // low, dtype=jnp.int32)
    lo_ids = jnp.arange(low, dtype=jnp.int32)
    hi_re, hi_im = unit_circle(hi_ids[:, None] * col_ids, SAMP)
    lo_re, lo_im = unit_circle(lo_ids[:, None] * col_ids, SAMP)
    hi_re, hi_im, lo_re, lo_im = lax.optimization_barrier((hi_re, hi_im, lo_re, lo_im))
    scale = 1.0 / math.sqrt(SAMP)
    real = (hi_re[:, None] * lo_re[None] - hi_im[:, None] * lo_im[None]) * scale
    imag = (hi_re[:, None] * lo_im[None] + hi_im[:, None] * lo_re[None]) * -scale
    return jnp.concatenate(
        [real.reshape(count, SAMP), imag.reshape(count, SAMP)], axis=0
    ).astype(jnp.bfloat16)


def beam_sums(block, member, first_channel, east_ids):
    per, _, _, frames, _ = block.shape
    ids = jnp.arange(NS_FEEDS, dtype=jnp.int32)
    outer = ids[:, None] * ids[None, :]
    whole = 2 * C * NS_FEEDS
    span, low = min(per, 32), 8
    lo_re, lo_im = unit_circle(-outer[None] * jnp.arange(low, dtype=jnp.int32)[:, None, None], whole)
    def add_chunk(chunk_at, total):
        start = chunk_at * span
        at = 2 * C - first_channel - start - low * jnp.arange(span // low, dtype=jnp.int32)
        hi_re, hi_im = unit_circle(outer[None] * at[:, None, None], whole)
        hi_re, hi_im = lax.optimization_barrier((hi_re, hi_im))
        w_re = hi_re[:, None] * lo_re[None] - hi_im[:, None] * lo_im[None]
        w_im = hi_re[:, None] * lo_im[None] + hi_im[:, None] * lo_re[None]
        weights = jnp.concatenate([w_re, w_im], axis=3).astype(jnp.bfloat16)
        weights = lax.optimization_barrier(weights.reshape(span, NS_FEEDS, 2 * NS_FEEDS))
        rows = lax.dynamic_slice_in_dim(block, start, span).reshape(span, EW_FEEDS * 2 * frames, NS_FEEDS)
        products = lax.dot_general(
            rows, weights, (((2,), (1,)), ((0,), (0,))), preferred_element_type=jnp.float32
        ).reshape(span, EW_FEEDS, 2, frames, 2 * NS_FEEDS)
        y_re = products[:, :, 0, :, :NS_FEEDS] - products[:, :, 1, :, NS_FEEDS:]
        y_im = products[:, :, 0, :, NS_FEEDS:] + products[:, :, 1, :, :NS_FEEDS]
        freqs = 2 * C - first_channel - start - jnp.arange(span, dtype=jnp.int32)
        powers = []
        for beam in range(EW_FEEDS):
            t_re, t_im = unit_circle(
                freqs[:, None] * (beam * east_ids)[None, :], 2 * C * EW_FEEDS
            )
            sum_re, sum_im = 0.0, 0.0
            for east in range(EW_FEEDS):
                c_re, c_im = t_re[:, east, None, None], t_im[:, east, None, None]
                sum_re = sum_re + (y_re[:, east] * c_re - y_im[:, east] * c_im)
                sum_im = sum_im + (y_re[:, east] * c_im + y_im[:, east] * c_re)
            powers.append(sum_re * sum_re + sum_im * sum_im)
        power = jnp.concatenate(powers, axis=2)
        return total + jnp.einsum(
            "cs,cfb->sfb", lax.dynamic_slice_in_dim(member, start, span), power, precision=lax.Precision.HIGHEST
        )

    zeros = jnp.zeros((member.shape[1], frames, BEAMS), jnp.float32)
    return lax.fori_loop(0, per // span, add_chunk, zeros)


def dedisperse(centered, delays):
    subs, total_frames, beams = centered.shape
    trials = delays.shape[0]
    frame_ids = jnp.arange(total_frames, dtype=jnp.int32)
    key = (frame_ids[None, :, None] + jnp.transpose(delays)[:, None, :]) % total_frames
    pick = (key[:, :, None, :] == frame_ids[None, None, :, None]).astype(jnp.float32)
    shares = jnp.einsum("smb,smtd->btd", centered, pick, precision=lax.Precision.HIGHEST)
    return jnp.transpose(shares, (1, 0, 2)) * (1.0 / math.sqrt(C))


def local(voltages, steering, chan_sub, delays):
    groups = lax.axis_size("grp")
    bands = lax.axis_size("band")
    grp_at = lax.axis_index("grp")
    frames, inputs, samples = voltages.shape
    local_beams = BEAMS // groups
    local_subs = delays.shape[1]
    part = groups // POLS
    per = C // part
    first_channel = grp_at % part * per
    place = grp_at % part

    rim_rows = shifted(voltages[frames - 3 :], "band", 1)
    trials = delays.shape[0] // bands
    quarter_chans = chan_sub.shape[0]
    lists = jnp.concatenate(
        [
            delays.reshape(bands, trials * local_subs),
            jnp.broadcast_to(chan_sub[None, :], (bands, quarter_chans)),
        ],
        axis=1,
    )
    lists = lax.all_to_all(lists, "band", split_axis=0, concat_axis=0, tiled=True)
    own_delays = lists[:, : trials * local_subs].reshape(bands, trials, local_subs)
    own_delays = jnp.transpose(own_delays, (1, 0, 2)).reshape(trials, bands * local_subs)
    every_chan_sub = lists[:, trials * local_subs :].reshape(C)
    window = window_taps()
    tables = [lax.optimization_barrier(dft_rows((place ^ hop) * per, per)) for hop in range(part)]

    def exchanged(first):
        if first >= 3:
            padded = voltages[first - 3 : first + GROUP_FRAMES]
        else:
            padded = jnp.concatenate([rim_rows, voltages[:GROUP_FRAMES]], axis=0)
        filtered = window[0][None, None, :] * padded[0:GROUP_FRAMES].astype(jnp.float32)
        for tap_at in range(1, 4):
            filtered = filtered + window[tap_at][None, None, :] * padded[
                tap_at : tap_at + GROUP_FRAMES
            ].astype(jnp.float32)
        filtered = lax.optimization_barrier(
            filtered.astype(jnp.bfloat16).reshape(GROUP_FRAMES * inputs, samples)
        )
        turned = []
        for hop in list(range(1, part)) + [0]:
            spectra = lax.dot_general(
                tables[hop], filtered, (((1,), (1,)), ((), ())), preferred_element_type=jnp.float32
            ).astype(jnp.bfloat16)
            if hop:
                spectra = lax.ppermute(spectra, "grp", [(i, i ^ hop) for i in range(groups)])
            turned.append(spectra.reshape(2, per, GROUP_FRAMES * inputs))
        turned = turned[-1:] + turned[:-1]
        pieces = NS_FEEDS // inputs
        if pieces == 1:
            return turned
        turned = jnp.stack(turned)[place ^ jnp.arange(part, dtype=jnp.int32)]
        turned = turned.reshape(EW_FEEDS, pieces, 2, per, GROUP_FRAMES, inputs)
        turned = jnp.transpose(turned, (0, 2, 3, 4, 1, 5))
        turned = turned.reshape(EW_FEEDS, 2, per, GROUP_FRAMES * NS_FEEDS)
        return [turned[east] for east in range(EW_FEEDS)]

    firsts = list(range(GROUP_FRAMES, frames, GROUP_FRAMES)) + [0]
    turned = {first: exchanged(first) for first in firsts}
    received = [block for first in sorted(firsts) for block in turned[first]]
    east_ids = jnp.arange(EW_FEEDS, dtype=jnp.int32)
    if inputs == NS_FEEDS:
        east_ids = place ^ east_ids

    subs = lax.dynamic_slice_in_dim(every_chan_sub, first_channel, per) % local_subs
    member = (subs[:, None] == jnp.arange(local_subs, dtype=jnp.int32)[None, :]).astype(jnp.float32)
    groups_of = frames // GROUP_FRAMES
    block = jnp.stack(received).reshape(
        groups_of, EW_FEEDS, 2, per, GROUP_FRAMES, NS_FEEDS
    )
    block = jnp.transpose(block, (3, 1, 2, 0, 4, 5)).reshape(
        per, EW_FEEDS, 2, frames, NS_FEEDS
    )
    sums = beam_sums(block, member, first_channel, east_ids)
    grid_ids = jnp.arange(BEAMS, dtype=jnp.int32)
    beam_place = steering[1] * NS_FEEDS + steering[0]
    pick = (grid_ids[:, None] == beam_place[None, :]).astype(jnp.float32)
    ordered = jnp.dot(
        sums.reshape(local_subs * frames, BEAMS),
        pick,
        precision=lax.Precision.HIGHEST,
        preferred_element_type=jnp.float32,
    ) * (1.0 / FEEDS)
    by_owner = lax.all_to_all(
        ordered.reshape(local_subs, frames, groups, local_beams),
        "grp",
        split_axis=2,
        concat_axis=0,
    )
    own_sums = jnp.sum(
        by_owner.reshape(
            POLS, QUARTERS, part // QUARTERS, local_subs, frames, local_beams
        ),
        axis=(0, 2),
    ).reshape(QUARTERS * local_subs, frames, local_beams)
    every_frame = lax.all_gather(own_sums, "band", axis=0, tiled=True)
    every_frame = every_frame.reshape(bands, -1, frames, local_beams)
    every_frame = jnp.transpose(every_frame, (1, 0, 2, 3)).reshape(-1, bands * frames, local_beams)
    centered = every_frame - jnp.mean(every_frame, axis=1, keepdims=True)
    return dedisperse(centered, own_delays)


def solution(mesh):
    in_specs = (P("band", "grp", None), P(), P("band"), P(None, "band"))
    out_specs = P(None, "grp", "band")
    return jax.shard_map(local, mesh=mesh, in_specs=in_specs, out_specs=out_specs, check_vma=False)
```
